512 devices in a mesh: dp: 32 (over z, x), cent: 16 (over y, core).
Axes of the slice: x: 4, y: 8, z: 8, core: 2. Of those that a mesh axis runs over, the one named last changes fastest.
Arguments:
- embeds: bfloat16 [262144, 768], P(('dp', 'cent')), may hold values from -6 to 6
- coarse_ids: int32 [262144], P(('dp', 'cent')), may hold values from 0 to 127, as said below
- fine_ids: int32 [262144], P(('dp', 'cent')), may hold values from 0 to 16383, as said below
- coarse_cents: float32 [128, 768], replicated, may hold values from -3 to 3
- fine_cents: bfloat16 [128, 128, 768], P('cent'), may hold values from -3 to 3
Outputs:
- new_fine: float32 [128, 128, 768], P('cent', 'dp')
- new_coarse: float32 [128, 768], replicated
- fine_gaps: float32 [262144], P(('dp', 'cent'))
The draws below stay inside these ranges and needn't reach their ends.
Inputs may be any that keep to these rules, and one draw needn't show every extreme that they name: `coarse_ids`: the coarse cluster c is owned by index c // 8 of cent. The embeddings of one device (each aligned block of 512 rows) fall in exactly 8 coarse clusters, no two with the same owner; at most 128 embeddings of one device lie in one cluster, and on every device one cluster holds exactly 128. fine_ids[r] // 128 equals coarse_ids[r].
All inputs are finite; a program needn't handle non-finite values.
Results may differ from the reference program's by a relative error of at most 0.00035.
Values may be sent and summed in bfloat16 or wider, within the bound.
No kernel may reach another device: no remote copies, remote signals or barrier semaphores. Data moves between devices by JAX's collectives and lax.ppermute only.
A program may use at most 64 MiB of HBM per device.

```python
import jax
import jax.numpy as jnp
from jax import lax

D = 768
COARSE = 128
FP = 128
ROWS_DEV = 512
ROWS = 262144
BLK_DEV = 8
SLOTS = 8
RCAP = 128
ANCHOR_C = 2048
ANCHOR_F = 16


def clusters(key):
    groups = ROWS // ROWS_DEV
    keys = jax.random.split(key, groups)

    def one_device(sub):
        first, second, third, fourth = jax.random.split(sub, 4)
        owner_list = jax.random.permutation(first, COARSE // BLK_DEV)[:SLOTS].astype(jnp.int32)
        picks = owner_list * BLK_DEV + jax.random.randint(second, (SLOTS,), 0, BLK_DEV).astype(jnp.int32)
        pool = 1 + jnp.arange((SLOTS - 1) * RCAP, dtype=jnp.int32) // RCAP
        remain = jax.random.permutation(third, pool)[:ROWS_DEV - RCAP]
        labels = jnp.concatenate([jnp.zeros((RCAP,), jnp.int32), remain.astype(jnp.int32)])
        labels = jax.random.permutation(fourth, labels)
        return picks[labels]
    return jax.vmap(one_device)(keys).reshape(ROWS).astype(jnp.int32)


def draw_coarse_ids(key, part):
    shared = clusters(key)
    return shared


def draw_fine_ids(key, part):
    shared = clusters(key)
    key = jax.random.fold_in(key, 5)
    within = jax.random.randint(key, (ROWS,), 0, FP).astype(jnp.int32)
    return (shared * FP + within).astype(jnp.int32)


def shard_levels(key, shape, cuts, least, high):
    def one(position, parts):
        draws = jax.random.uniform(jax.random.fold_in(jax.random.fold_in(key, 6), position), (parts,), jnp.float32, least / len(cuts), high / len(cuts))
        return jnp.repeat(jnp.exp(draws), shape[position] // parts).reshape((-1,) + (1,) * (len(shape) - position - 1))

    gain = one(*cuts[0])
    for cut in cuts[1:]:
        gain = gain * one(*cut)
    return gain


def bell_draw(stream_key, shape, width, most, cuts=(), kind=jnp.bfloat16):
    result = width * jax.random.normal(stream_key, shape, jnp.float32)
    if cuts:
        result = result * shard_levels(stream_key, shape, cuts, -0.22, 0.18)
    return jnp.clip(result, -most, most).astype(kind)


def setup_inputs(seed: int = 0) -> dict:
    arg_keys = jax.random.split(jax.random.key(seed), 6)
    embeds = bell_draw(arg_keys[0], (ROWS, D), 1.0, 6.0, ((0, 512),))
    coarse_ids = draw_coarse_ids(jax.random.fold_in(arg_keys[5], 71), 0)
    fine_ids = draw_fine_ids(jax.random.fold_in(arg_keys[5], 71), 0)
    coarse_cents = bell_draw(arg_keys[3], (COARSE, D), 0.5, 3.0, (), jnp.float32)
    fine_cents = bell_draw(arg_keys[4], (COARSE, FP, D), 0.5, 3.0, ((0, 16),))
    return dict(embeds=embeds, coarse_ids=coarse_ids, fine_ids=fine_ids, coarse_cents=coarse_cents, fine_cents=fine_cents)


def reference(embeds, coarse_ids, fine_ids, coarse_cents, fine_cents):
    fine_sq = jnp.sum(jnp.square(fine_cents.astype(jnp.float32)), axis=2)

    def gap_block(args):
        rows, ids = args
        rows32 = rows.astype(jnp.float32)
        blocks = fine_cents[ids].astype(jnp.float32)
        dots = jnp.einsum("rd,rfd->rf", rows32, blocks, precision=lax.Precision.HIGHEST)
        row_sq = jnp.sum(rows32 * rows32, axis=1)
        dist = (row_sq[:, None] - 2.0 * dots + fine_sq[ids]) / D
        return jnp.min(dist, axis=1)

    groups = ROWS // ROWS_DEV
    fine_gaps = lax.map(gap_block, (embeds.reshape(groups, ROWS_DEV, D), coarse_ids.reshape(groups, ROWS_DEV))).reshape(ROWS)

    def add_block(carry, args):
        rows, cids, fids = args
        rows32 = rows.astype(jnp.float32)
        ones = jnp.ones((rows.shape[0],), jnp.float32)
        coarse_sum, coarse_count, fine_sum, fine_count = carry
        coarse_sum = coarse_sum + jax.ops.segment_sum(rows32, cids, COARSE)
        coarse_count = coarse_count + jax.ops.segment_sum(ones, cids, COARSE)
        fine_sum = fine_sum + jax.ops.segment_sum(rows32, fids, COARSE * FP)
        fine_count = fine_count + jax.ops.segment_sum(ones, fids, COARSE * FP)
        return (coarse_sum, coarse_count, fine_sum, fine_count), None

    start = (jnp.zeros((COARSE, D), jnp.float32), jnp.zeros((COARSE,), jnp.float32),
             jnp.zeros((COARSE * FP, D), jnp.float32), jnp.zeros((COARSE * FP,), jnp.float32))
    totals, unused = lax.scan(add_block, start, (embeds.reshape(groups, ROWS_DEV, D), coarse_ids.reshape(groups, ROWS_DEV), fine_ids.reshape(groups, ROWS_DEV)))
    coarse_sum, coarse_count, fine_sum, fine_count = totals
    new_coarse = (ANCHOR_C * coarse_cents + coarse_sum) / (ANCHOR_C + coarse_count[:, None])
    fine_sum = fine_sum.reshape(COARSE, FP, D)
    fine_count = fine_count.reshape(COARSE, FP)
    new_fine = (ANCHOR_F * fine_cents.astype(jnp.float32) + fine_sum) / (ANCHOR_F + fine_count[:, :, None])
    return new_fine, new_coarse, fine_gaps
```

```python
import functools

import jax
import jax.numpy as jnp
from jax import lax
from jax.experimental import pallas as pl
from jax.experimental.pallas import tpu as pltpu
from jax.sharding import Mesh, PartitionSpec as P

COARSE = 128
DP = ("z", "x")
CENT = ("y", "core")
PARTS = 3


def sums_kernel(pick, key_ref, target_ref, rows_ref, out_ref):
    source = pl.program_id(0)

    @pl.when(source == 0)
    def _():
        out_ref[...] = jnp.zeros_like(out_ref)

    hot = (target_ref[...] == key_ref[0]).astype(jnp.bfloat16)
    part = jnp.dot(hot, rows_ref[0], preferred_element_type=jnp.float32)
    pair = pick[source] // 2
    out_ref[:, pair] += part.reshape(out_ref.shape[0], 8, part.shape[1])


def fine_sums(pick, keys, target, rows, per_source):
    sources, _, width = rows.shape
    groups = target.shape[0] // 8
    pairs = 4
    return pl.pallas_call(
        sums_kernel,
        grid_spec=pltpu.PrefetchScalarGridSpec(
            num_scalar_prefetch=1,
            grid=(sources,),
            in_specs=[
                pl.BlockSpec((1, 1, per_source), lambda s, pick: (s, 0, 0)),
                pl.BlockSpec((groups * 8, 1), lambda s, pick: (0, 0)),
                pl.BlockSpec((1, per_source, width), lambda s, pick: (s, 0, 0)),
            ],
            out_specs=pl.BlockSpec((groups, pairs, 8, width), lambda s, pick: (0, 0, 0, 0)),
        ),
        out_shape=jax.ShapeDtypeStruct((groups, pairs, 8, width), jnp.float32),
        compiler_params=pltpu.CompilerParams(vmem_limit_bytes=32 * 2**20),
    )(pick, keys, target, rows)


def gaps_kernel(pick, cents_ref, square_ref, *refs):
    out_ref = refs[-1]
    dots = None
    start = 0
    for rows_ref in refs[:-1]:
        width = rows_ref.shape[2]
        term = lax.dot_general(
            cents_ref[0, :, start : start + width],
            rows_ref[0],
            (((1,), (1,)), ((), ())),
            preferred_element_type=jnp.float32,
        )
        dots = term if dots is None else dots + term
        start += width
    out_ref[0] = jnp.min(square_ref[0] - 2.0 * dots, axis=0, keepdims=True)


def nearest(pick, cents, squares, rows, per_source):
    sources = rows[0].shape[0]
    per, width = cents.shape[1:]
    return pl.pallas_call(
        gaps_kernel,
        grid_spec=pltpu.PrefetchScalarGridSpec(
            num_scalar_prefetch=1,
            grid=(sources,),
            in_specs=[
                pl.BlockSpec((1, per, width), lambda s, pick: (pick[s], 0, 0)),
                pl.BlockSpec((1, per, 1), lambda s, pick: (pick[s], 0, 0)),
            ]
            + [pl.BlockSpec((1, per_source, r.shape[2]), lambda s, pick: (s, 0, 0)) for r in rows],
            out_specs=pl.BlockSpec((1, 1, per_source), lambda s, pick: (s, 0, 0)),
        ),
        out_shape=jax.ShapeDtypeStruct((sources, 1, per_source), jnp.float32),
        compiler_params=pltpu.CompilerParams(vmem_limit_bytes=32 * 2**20),
    )(pick, cents, squares, *rows)


def body(embeds, coarse_ids, fine_ids, coarse_cents, fine_cents):
    blk, per, width = fine_cents.shape
    count = embeds.shape[0]
    depth, across = lax.axis_size("z"), lax.axis_size("x")
    planes = depth * across
    owners = lax.axis_size(CENT)
    share = per // planes
    me = lax.axis_index(CENT)
    anchor_coarse = count * planes * owners // COARSE
    anchor_fine = max(1, anchor_coarse // per)
    local = fine_ids - coarse_ids * per
    piece = width // PARTS

    ids = jnp.concatenate([coarse_ids, local]).astype(jnp.bfloat16).reshape(-1, piece)
    ids = jnp.pad(ids, ((0, 16 - ids.shape[0]), (0, 0)))
    gathered = []
    for k in range(PARTS):
        block = embeds[:, k * piece : (k + 1) * piece]
        if k == 0:
            block = jnp.concatenate([block, ids], axis=0)
        gathered.append(lax.all_gather(block, CENT, axis=0, tiled=False))

    coarse_hot = (jnp.arange(COARSE, dtype=jnp.int32)[:, None] == coarse_ids[None, :]).astype(jnp.bfloat16)
    fine_hot = (local[:, None] == jnp.arange(per, dtype=jnp.int32)[None, :]).astype(jnp.bfloat16)
    coarse_part = jnp.dot(
        coarse_hot, jnp.concatenate([embeds, fine_hot], axis=1), preferred_element_type=jnp.float32
    )
    coarse_part = coarse_part.reshape(planes, COARSE // planes, width + per)
    mine = jnp.sum(lax.all_to_all(coarse_part, DP, split_axis=0, concat_axis=0, tiled=True), axis=0)
    mine = jnp.sum(lax.all_gather(mine, CENT, axis=0, tiled=False), axis=0)
    totals = lax.all_to_all(
        jnp.broadcast_to(mine[None], (planes,) + mine.shape), DP, split_axis=0, concat_axis=0, tiled=True
    ).reshape(COARSE, width + per)
    counts = totals[:, width:]
    new_coarse = (anchor_coarse * coarse_cents + totals[:, :width]) / (
        anchor_coarse + jnp.sum(counts, axis=1, keepdims=True)
    )

    sent = gathered[0][:, count : count + 2 * count // piece, :].reshape(owners, 2, count).astype(jnp.int32)
    cluster = sent[:, 0] - me * blk
    ours = (cluster >= 0) & (cluster < blk)
    pick = jnp.max(jnp.where(ours, cluster, 0), axis=1)
    keys = jnp.where(ours, (cluster % 2) * per + sent[:, 1], -1)[:, None, :]
    slot = jnp.arange(2 * per, dtype=jnp.int32)
    group, half, inner = slot // (2 * share), (slot // share) % 2, slot % share
    target = (half * per + (group % depth) * across * share + (group // depth) * share + inner)[:, None]

    fine_parts = []
    for k in range(PARTS):
        part = fine_sums(pick, keys, target, gathered[k], count).reshape(across, depth, blk * share, piece)
        part = jnp.sum(lax.all_to_all(part, "x", split_axis=0, concat_axis=0, tiled=True), axis=0)
        part = jnp.sum(lax.all_to_all(part, "z", split_axis=0, concat_axis=0, tiled=True), axis=0)
        fine_parts.append(part.reshape(blk, share, piece))
    fine_sum = jnp.concatenate(fine_parts, axis=2)
    first = lax.axis_index(DP) * share
    former = lax.dynamic_slice_in_dim(fine_cents, first, share, 1).astype(jnp.float32)
    fine_num = lax.dynamic_slice(counts, (me * blk, first), (blk, share))
    new_fine = (anchor_fine * former + fine_sum) / (anchor_fine + fine_num[:, :, None])

    squares = jnp.sum(jnp.square(fine_cents.astype(jnp.float32)), axis=2, keepdims=True)
    least = nearest(pick, fine_cents, squares, gathered, count)
    back = lax.all_to_all(least, CENT, split_axis=0, concat_axis=0, tiled=True)[:, 0]
    row_sq = jnp.sum(jnp.square(embeds.astype(jnp.float32)), axis=1)
    at = (coarse_ids // blk)[None, :] == jnp.arange(owners, dtype=jnp.int32)[:, None]
    gaps = (row_sq + jnp.sum(jnp.where(at, back, 0.0), axis=0)) / width
    return (new_fine, new_coarse, gaps)


def solution(mesh):
    fine_mesh = Mesh(mesh.devices.reshape(8, 4, 8, 2), DP + CENT)
    placed = (P(DP + CENT, None), P(DP + CENT), P(DP + CENT), P(), P(CENT, None, None))
    return jax.shard_map(
        body,
        mesh=fine_mesh,
        in_specs=placed,
        out_specs=(P(CENT, DP, None), P(), P(DP + CENT)),
        check_vma=False,
    )
```

```python
import jax
import jax.numpy as jnp
from jax import lax
from jax.experimental import pallas as pl
from jax.experimental.pallas import tpu as pltpu
from jax.sharding import Mesh, PartitionSpec as P

COARSE = 128
DP = ("z", "x")
CENT = ("y", "core")
VMEM = 56 * 2**20


def sums_kernel(pick, key_ref, target_ref, rows_ref, out_ref):
    source = pl.program_id(0)

    @pl.when(source == 0)
    def _():
        out_ref[...] = jnp.zeros_like(out_ref)

    hot = (target_ref[...] == key_ref[0]).astype(jnp.bfloat16)
    part = jnp.dot(hot, rows_ref[0], preferred_element_type=jnp.float32)
    pair = pick[source] // 2
    out_ref[:, pair] += part.reshape(out_ref.shape[0], 8, part.shape[1])


def fine_sums(pick, keys, target, rows):
    sources, per_source, width = rows.shape
    groups = target.shape[0] // 8
    shape = (groups, 4, 8, width)
    return pl.pallas_call(
        sums_kernel,
        grid_spec=pltpu.PrefetchScalarGridSpec(
            num_scalar_prefetch=1,
            grid=(sources,),
            in_specs=[
                pl.BlockSpec((1, 1, per_source), lambda s, pick: (s, 0, 0)),
                pl.BlockSpec((groups * 8, 1), lambda s, pick: (0, 0)),
                pl.BlockSpec((1, per_source, width), lambda s, pick: (s, 0, 0)),
            ],
            out_specs=pl.BlockSpec(shape, lambda s, pick: (0, 0, 0, 0)),
        ),
        out_shape=jax.ShapeDtypeStruct(shape, jnp.float32),
        compiler_params=pltpu.CompilerParams(vmem_limit_bytes=VMEM),
        cost_estimate=pl.CostEstimate(
            flops=4 * groups * 4 * rows.size, bytes_accessed=2 * rows.size, transcendentals=0
        ),
    )(pick, keys, target, rows)


def gaps_kernel(pick, cents_ref, square_ref, rows_ref, out_ref):
    dots = lax.dot_general(
        cents_ref[0], rows_ref[0], (((1,), (1,)), ((), ())), preferred_element_type=jnp.float32
    )
    out_ref[0] = jnp.min(square_ref[0] - 2.0 * dots, axis=0, keepdims=True)


def nearest(pick, cents, squares, rows):
    sources, per_source, width = rows.shape
    per = cents.shape[1]
    return pl.pallas_call(
        gaps_kernel,
        grid_spec=pltpu.PrefetchScalarGridSpec(
            num_scalar_prefetch=1,
            grid=(sources,),
            in_specs=[
                pl.BlockSpec((1, per, width), lambda s, pick: (pick[s], 0, 0)),
                pl.BlockSpec((1, per, 1), lambda s, pick: (pick[s], 0, 0)),
                pl.BlockSpec((1, per_source, width), lambda s, pick: (s, 0, 0)),
            ],
            out_specs=pl.BlockSpec((1, 1, per_source), lambda s, pick: (s, 0, 0)),
        ),
        out_shape=jax.ShapeDtypeStruct((sources, 1, per_source), jnp.float32),
        compiler_params=pltpu.CompilerParams(vmem_limit_bytes=VMEM),
        cost_estimate=pl.CostEstimate(
            flops=2 * per * rows.size, bytes_accessed=2 * rows.size, transcendentals=0
        ),
    )(pick, cents, squares, rows)


def body(embeds, coarse_ids, fine_ids, coarse_cents, fine_cents):
    blk, per, width = fine_cents.shape
    count = embeds.shape[0]
    depth, across = lax.axis_size("z"), lax.axis_size("x")
    planes = depth * across
    owners = lax.axis_size(CENT)
    share = per // planes
    me = lax.axis_index(CENT)
    anchor_coarse = count * planes * owners // COARSE
    anchor_fine = max(1, anchor_coarse // per)
    local = fine_ids - coarse_ids * per

    rows = lax.all_gather(embeds, CENT, axis=0, tiled=False)
    sent = lax.all_gather(fine_ids, CENT, axis=0, tiled=False)

    coarse_hot = (jnp.arange(COARSE, dtype=jnp.int32)[:, None] == coarse_ids[None, :]).astype(jnp.bfloat16)
    fine_hot = (local[:, None] == jnp.arange(per, dtype=jnp.int32)[None, :]).astype(jnp.bfloat16)
    coarse_part = jnp.dot(
        coarse_hot, jnp.concatenate([embeds, fine_hot], axis=1), preferred_element_type=jnp.float32
    )
    coarse_part = coarse_part.reshape(planes, COARSE // planes, width + per)
    mine = jnp.sum(lax.all_to_all(coarse_part, DP, split_axis=0, concat_axis=0, tiled=True), axis=0)
    mine = jnp.sum(lax.all_gather(mine, CENT, axis=0, tiled=False), axis=0)
    totals = lax.all_to_all(
        jnp.broadcast_to(mine[None], (planes,) + mine.shape), DP, split_axis=0, concat_axis=0, tiled=True
    ).reshape(COARSE, width + per)
    counts = totals[:, width:]
    new_coarse = (anchor_coarse * coarse_cents + totals[:, :width]) / (
        anchor_coarse + jnp.sum(counts, axis=1, keepdims=True)
    )

    cluster = sent // per - me * blk
    ours = (cluster >= 0) & (cluster < blk)
    pick = jnp.max(jnp.where(ours, cluster, 0), axis=1)
    keys = jnp.where(ours, sent % (2 * per), -1)[:, None, :]
    slot = jnp.arange(2 * per, dtype=jnp.int32)
    group, half, inner = slot // (2 * share), (slot // share) % 2, slot % share
    target = (half * per + (group % depth) * across * share + (group // depth) * share + inner)[:, None]

    part = fine_sums(pick, keys, target, rows).reshape(across, depth, blk * share, width)
    part = jnp.sum(lax.all_to_all(part, "x", split_axis=0, concat_axis=0, tiled=True), axis=0)
    part = jnp.sum(lax.all_to_all(part, "z", split_axis=0, concat_axis=0, tiled=True), axis=0)
    fine_sum = part.reshape(blk, share, width)
    first = lax.axis_index(DP) * share
    former = lax.dynamic_slice_in_dim(fine_cents, first, share, 1).astype(jnp.float32)
    fine_num = lax.dynamic_slice(counts, (me * blk, first), (blk, share))
    new_fine = (anchor_fine * former + fine_sum) / (anchor_fine + fine_num[:, :, None])

    squares = jnp.sum(jnp.square(fine_cents.astype(jnp.float32)), axis=2, keepdims=True)
    least = nearest(pick, fine_cents, squares, rows)
    back = lax.all_to_all(least, CENT, split_axis=0, concat_axis=0, tiled=True)[:, 0]
    row_sq = jnp.sum(jnp.square(embeds.astype(jnp.float32)), axis=1)
    at = (coarse_ids // blk)[None, :] == jnp.arange(owners, dtype=jnp.int32)[:, None]
    gaps = (row_sq + jnp.sum(jnp.where(at, back, 0.0), axis=0)) / width
    return (new_fine, new_coarse, gaps)


def solution(mesh):
    fine_mesh = Mesh(mesh.devices.reshape(8, 4, 8, 2), DP + CENT)
    placed = (P(DP + CENT, None), P(DP + CENT), P(DP + CENT), P(), P(CENT, None, None))
    return jax.shard_map(
        body,
        mesh=fine_mesh,
        in_specs=placed,
        out_specs=(P(CENT, DP, None), P(), P(DP + CENT)),
        check_vma=False,
    )
```

```python
import jax
import jax.numpy as jnp
from jax import lax
from jax.experimental import pallas as pl
from jax.experimental.pallas import tpu as pltpu
from jax.sharding import Mesh, PartitionSpec as P

COARSE = 128
DP = ("z", "x")
CENT = ("y", "core")
VMEM = 56 * 2**20


def sums_kernel(pick_ref, key_ref, target_ref, rows_ref, total, held, sems):
    sources = rows_ref.shape[0]

    def fetch(s):
        return pltpu.make_async_copy(rows_ref.at[s], held.at[s], sems.at[s])

    for s in range(sources):
        fetch(s).start()
    total[...] = jnp.zeros_like(total)

    @pl.loop(0, sources)
    def _(s):
        hot = (target_ref[...] == key_ref[s]).astype(jnp.bfloat16)
        fetch(s).wait()
        part = jnp.dot(hot, held[s], preferred_element_type=jnp.float32)
        total[:, pick_ref[s] // 2] += part.reshape(total.shape[0], 8, part.shape[1])


def fine_sums(pick, keys, target, rows):
    sources, per_source, width = rows.shape
    groups = target.shape[0] // 8
    shape = (groups, 4, 8, width)
    return pl.pallas_call(
        sums_kernel,
        in_specs=[
            pl.BlockSpec(memory_space=pltpu.SMEM),
            pl.BlockSpec(memory_space=pltpu.VMEM),
            pl.BlockSpec(memory_space=pltpu.VMEM),
            pl.BlockSpec(memory_space=pl.ANY),
        ],
        out_specs=pl.BlockSpec(memory_space=pltpu.VMEM),
        out_shape=jax.ShapeDtypeStruct(shape, jnp.float32),
        scratch_shapes=[
            pltpu.VMEM(rows.shape, rows.dtype),
            pltpu.SemaphoreType.DMA((sources,)),
        ],
        compiler_params=pltpu.CompilerParams(vmem_limit_bytes=VMEM),
        cost_estimate=pl.CostEstimate(
            flops=4 * groups * 4 * rows.size, bytes_accessed=2 * rows.size, transcendentals=0
        ),
    )(pick, keys, target, rows)


def gaps_kernel(pick_ref, cents_ref, square_ref, rows_ref, out_ref, held, sems):
    sources = rows_ref.shape[0]

    def fetch(s):
        return pltpu.make_async_copy(rows_ref.at[s], held.at[s], sems.at[s])

    for s in range(sources):
        fetch(s).start()

    @pl.loop(0, sources)
    def _(s):
        c = pick_ref[s]
        fetch(s).wait()
        dots = lax.dot_general(
            cents_ref[c], held[s], (((1,), (1,)), ((), ())), preferred_element_type=jnp.float32
        )
        out_ref[s] = jnp.min(square_ref[c] - 2.0 * dots, axis=0, keepdims=True)


def nearest(pick, cents, squares, rows):
    sources, per_source, width = rows.shape
    return pl.pallas_call(
        gaps_kernel,
        in_specs=[
            pl.BlockSpec(memory_space=pltpu.SMEM),
            pl.BlockSpec(memory_space=pltpu.VMEM),
            pl.BlockSpec(memory_space=pltpu.VMEM),
            pl.BlockSpec(memory_space=pl.ANY),
        ],
        out_specs=pl.BlockSpec(memory_space=pltpu.VMEM),
        out_shape=jax.ShapeDtypeStruct((sources, 1, per_source), jnp.float32),
        scratch_shapes=[
            pltpu.VMEM(rows.shape, rows.dtype),
            pltpu.SemaphoreType.DMA((sources,)),
        ],
        compiler_params=pltpu.CompilerParams(vmem_limit_bytes=VMEM),
        cost_estimate=pl.CostEstimate(
            flops=2 * cents.shape[1] * rows.size, bytes_accessed=2 * rows.size, transcendentals=0
        ),
    )(pick, cents, squares, rows)


def body(embeds, coarse_ids, fine_ids, coarse_cents, fine_cents):
    blk, per, width = fine_cents.shape
    count = embeds.shape[0]
    planes = lax.axis_size(DP)
    owners = lax.axis_size(CENT)
    share = per // planes
    me = lax.axis_index(CENT)
    anchor_coarse = count * planes * owners // COARSE
    anchor_fine = max(1, anchor_coarse // per)
    local = fine_ids - coarse_ids * per

    rows = lax.all_gather(embeds, CENT, axis=0, tiled=False)
    sent = lax.all_gather(fine_ids, CENT, axis=0, tiled=False)

    coarse_hot = (jnp.arange(COARSE, dtype=jnp.int32)[:, None] == coarse_ids[None, :]).astype(jnp.bfloat16)
    fine_hot = (local[:, None] == jnp.arange(per, dtype=jnp.int32)[None, :]).astype(jnp.bfloat16)
    coarse_part = jnp.dot(
        coarse_hot, jnp.concatenate([embeds, fine_hot], axis=1), preferred_element_type=jnp.float32
    )
    largest = jnp.broadcast_to(jnp.max(jnp.abs(embeds)).astype(jnp.float32), (COARSE, 128))
    both = width + per
    coarse_part = jnp.concatenate([coarse_part, largest], axis=1).reshape(planes, COARSE // planes, both + 128)
    heard = lax.all_to_all(coarse_part, DP, split_axis=0, concat_axis=0, tiled=True)
    mine = jnp.concatenate([jnp.sum(heard[:, :, :both], axis=0), jnp.max(heard[:, :, both:], axis=0)], axis=1)
    heard = lax.all_gather(mine, CENT, axis=0, tiled=False)
    mine = jnp.sum(heard[:, :, :both], axis=0)
    largest = jnp.max(heard[:, :, both:])
    totals = lax.all_to_all(
        jnp.broadcast_to(mine[None], (planes,) + mine.shape), DP, split_axis=0, concat_axis=0, tiled=True
    ).reshape(COARSE, both)
    counts = totals[:, width:]
    new_coarse = (anchor_coarse * coarse_cents + totals[:, :width]) / (
        anchor_coarse + jnp.sum(counts, axis=1, keepdims=True)
    )

    powers = jnp.asarray([2.0**k for k in range(-8, 101)], jnp.float32)
    scale = jnp.max(jnp.where(powers * largest <= 60000.0 / (owners * 128), powers, powers[0]))

    cluster = sent // per - me * blk
    ours = (cluster >= 0) & (cluster < blk)
    pick = jnp.max(jnp.where(ours, cluster, 0), axis=1)
    keys = jnp.where(ours, sent % (2 * per), -1)[:, None, :]
    slot = jnp.arange(2 * per, dtype=jnp.int32)
    target = ((slot // share) % 2 * per + slot // (2 * share) * share + slot % share)[:, None]

    part = fine_sums(pick, keys, target, rows).reshape(planes, blk * share, width)
    part = (part * scale).astype(jnp.float16)
    part = lax.all_to_all(part, DP, split_axis=0, concat_axis=0, tiled=True)
    fine_sum = (jnp.sum(part.astype(jnp.float32), axis=0) * (1.0 / scale)).reshape(blk, share, width)
    first = lax.axis_index(DP) * share
    former = lax.dynamic_slice_in_dim(fine_cents, first, share, 1).astype(jnp.float32)
    fine_num = lax.dynamic_slice(counts, (me * blk, first), (blk, share))
    new_fine = (anchor_fine * former + fine_sum) / (anchor_fine + fine_num[:, :, None])

    squares = jnp.sum(jnp.square(fine_cents.astype(jnp.float32)), axis=2, keepdims=True)
    least = nearest(pick, fine_cents, squares, rows)[:, 0]
    back = lax.all_gather(least, CENT, axis=0, tiled=False)
    back = lax.dynamic_index_in_dim(back, me, 1, keepdims=False)
    row_sq = jnp.sum(jnp.square(embeds.astype(jnp.float32)), axis=1)
    at = (coarse_ids // blk)[None, :] == jnp.arange(owners, dtype=jnp.int32)[:, None]
    gaps = (row_sq + jnp.sum(jnp.where(at, back, 0.0), axis=0)) / width
    return (new_fine, new_coarse, gaps)


def solution(mesh):
    fine_mesh = Mesh(mesh.devices.reshape(8, 4, 8, 2), DP + CENT)
    placed = (P(DP + CENT, None), P(DP + CENT), P(DP + CENT), P(), P(CENT, None, None))
    return jax.shard_map(
        body,
        mesh=fine_mesh,
        in_specs=placed,
        out_specs=(P(CENT, DP, None), P(), P(DP + CENT)),
        check_vma=False,
    )
```

```python
import functools

import jax
import jax.numpy as jnp
from jax import lax
from jax.experimental import pallas as pl
from jax.experimental.pallas import tpu as pltpu
from jax.sharding import Mesh, PartitionSpec as P

COARSE = 128
DP = ("z", "x")
CENT = ("y", "core")
STEPS = 13
VMEM = 56 * 2**20


def message_kernel(share, owned, coarse_ref, fine_ref, rows_ref, out_ref):
    count, width = rows_ref.shape
    per = 128
    lines = out_ref.shape[0]
    slots, chunk = 8, 4
    full, half = share * width, width // 2
    coarse = coarse_ref[...]
    local = fine_ref[...] - coarse * per
    owner = coarse // owned

    owners = lax.broadcasted_iota(jnp.int32, (16, count), 0)
    present = jnp.max((owners == owner).astype(jnp.int32), axis=1, keepdims=True)
    slot_row = jnp.sum(jnp.where(owners < owner, present, 0), axis=0, keepdims=True)
    slot_ids = lax.broadcasted_iota(jnp.int32, (slots, count), 0)
    cluster = jnp.max(jnp.where(slot_ids == slot_row, coarse, 0), axis=1, keepdims=True)

    largest = jnp.max(jnp.abs(rows_ref[...]).astype(jnp.float32))
    scale, step = 1.0, 0.0
    for k in range(1, STEPS):
        fits = largest * 256.0**k <= 60000.0 / count
        scale = jnp.where(fits, 256.0**k, scale)
        step = jnp.where(fits, float(k), step)

    line = lax.broadcasted_iota(jnp.int32, (lines, 1), 0)
    key = slot_row * per + local
    target = (line % slots) * per + (line // slots) * share
    for j in range(share):
        hot = (target + j == key).astype(jnp.bfloat16)
        part = jnp.dot(hot, rows_ref[...], preferred_element_type=jnp.float32)
        out_ref[:, j * width : (j + 1) * width] = part * scale
    upper = line % slots < chunk
    hot = ((line // slots) * chunk + line % chunk == coarse).astype(jnp.bfloat16)
    part = jnp.dot(hot, rows_ref[...], preferred_element_type=jnp.float32)
    out_ref[:, full : full + half] = jnp.where(upper, part[:, :half], part[:, half:]) * scale
    fine_hot = (lax.broadcasted_iota(jnp.int32, (per, count), 0) == local).astype(jnp.bfloat16)
    numbers = lax.dot_general(hot, fine_hot, (((1,), (1,)), ((), ())), preferred_element_type=jnp.float32)
    lane = lax.broadcasted_iota(jnp.int32, (chunk, per), 1)
    cluster = cluster.astype(jnp.float32)
    notes = jnp.where(lane < 32, cluster[:chunk], jnp.where(lane < 64, cluster[chunk:], step))
    notes = jnp.concatenate([notes, notes], axis=0)
    notes = jnp.broadcast_to(notes[None], (lines // slots, slots, per)).reshape(lines, per)
    out_ref[:, full + half :] = jnp.where(upper, numbers, notes)


def message_of(coarse_ids, fine_ids, rows, planes, share, owned):
    width = rows.shape[1]
    shape = (planes * 8, share * width + width // 2 + 128)
    return pl.pallas_call(
        functools.partial(message_kernel, share, owned),
        in_specs=[pl.BlockSpec(memory_space=pltpu.VMEM)] * 3,
        out_specs=pl.BlockSpec(memory_space=pltpu.VMEM),
        out_shape=jax.ShapeDtypeStruct(shape, jnp.float32),
        compiler_params=pltpu.CompilerParams(vmem_limit_bytes=VMEM),
        cost_estimate=pl.CostEstimate(
            flops=2 * shape[0] * shape[1] * rows.shape[0], bytes_accessed=16 * rows.size, transcendentals=0
        ),
    )(coarse_ids[None, :], fine_ids[None, :], rows)


def gaps_kernel(pick_ref, cents_ref, square_ref, rows_ref, out_ref, held, sems):
    sources = rows_ref.shape[0]

    def fetch(s):
        return pltpu.make_async_copy(rows_ref.at[s], held.at[s], sems.at[s])

    for s in range(sources):
        fetch(s).start()

    @pl.loop(0, sources, unroll=4)
    def _(s):
        c = pick_ref[s]
        fetch(s).wait()
        dots = lax.dot_general(
            cents_ref[c], held[s], (((1,), (1,)), ((), ())), preferred_element_type=jnp.float32
        )
        out_ref[s] = jnp.min(square_ref[c] - 2.0 * dots, axis=0, keepdims=True)


def nearest(pick, cents, squares, rows):
    sources, per_source, width = rows.shape
    return pl.pallas_call(
        gaps_kernel,
        in_specs=[
            pl.BlockSpec(memory_space=pltpu.SMEM),
            pl.BlockSpec(memory_space=pltpu.VMEM),
            pl.BlockSpec(memory_space=pltpu.VMEM),
            pl.BlockSpec(memory_space=pl.ANY),
        ],
        out_specs=pl.BlockSpec(memory_space=pltpu.VMEM),
        out_shape=jax.ShapeDtypeStruct((sources, 1, per_source), jnp.float32),
        scratch_shapes=[
            pltpu.VMEM(rows.shape, rows.dtype),
            pltpu.SemaphoreType.DMA((sources,)),
        ],
        compiler_params=pltpu.CompilerParams(vmem_limit_bytes=VMEM),
        cost_estimate=pl.CostEstimate(
            flops=2 * cents.shape[1] * rows.size, bytes_accessed=2 * rows.size, transcendentals=0
        ),
    )(pick, cents, squares, rows)


def after(value, earlier):
    return value + (earlier[(0,) * earlier.ndim].astype(jnp.float32) * 0.0).astype(value.dtype)


def body(embeds, coarse_ids, fine_ids, coarse_cents, fine_cents):
    blk, per, width = fine_cents.shape
    count = embeds.shape[0]
    planes = lax.axis_size(DP)
    owners = lax.axis_size(CENT)
    share = per // planes
    chunk = COARSE // planes
    slots = 8
    me = lax.axis_index(CENT)
    core = lax.axis_index("core")
    anchor_coarse = count * planes * owners // COARSE
    anchor_fine = max(1, anchor_coarse // per)

    rows = lax.all_gather(embeds, CENT, axis=0, tiled=False)

    message = message_of(coarse_ids, fine_ids, embeds, planes, share, blk)
    heard = message.astype(jnp.float16).reshape(planes, slots, -1)
    heard = lax.all_to_all(heard, DP, split_axis=0, concat_axis=0, tiled=True)
    sent = lax.all_gather(after(coarse_ids, message), CENT, axis=0, tiled=False)

    full, half = share * width, width // 2
    notes = after(heard[:, chunk:, full + half :].astype(jnp.float32), sent)
    from_step = notes[:, 0, per - 1]
    from_cluster = jnp.concatenate([notes[:, :, 0], notes[:, :, 32]], axis=1).astype(jnp.int32)
    back_scale = jnp.zeros_like(from_step)
    for k in range(STEPS):
        back_scale = jnp.where(from_step == k, 256.0**-k, back_scale)
    weights = jnp.where(
        jnp.arange(COARSE, dtype=jnp.int32)[:, None, None] == from_cluster[None], back_scale[None, :, None], 0.0
    )
    weights = weights.reshape(COARSE, planes * slots).astype(jnp.bfloat16)
    values = heard[:, :, :full].reshape(planes * slots, full).astype(jnp.float32)
    high = lax.reduce_precision(values, 8, 7)
    low = (values - high).astype(jnp.bfloat16)
    high = high.astype(jnp.bfloat16)
    table = jnp.dot(weights, high, preferred_element_type=jnp.float32) + jnp.dot(
        weights, low, preferred_element_type=jnp.float32
    )

    rest = heard[:, :, full:].astype(jnp.float32)
    factor = jnp.where(jnp.arange(rest.shape[2])[None, None, :] < half, back_scale[:, None, None], 1.0)
    rest = jnp.sum(rest * factor, axis=0)

    table = table.reshape(owners // 2, 2, blk, full)
    kept = lax.dynamic_index_in_dim(table, core, 1, keepdims=False)
    given = lax.dynamic_index_in_dim(table, 1 - core, 1, keepdims=False)
    kept = jnp.concatenate([kept, jnp.broadcast_to(rest[None], (owners // 2,) + rest.shape)], axis=2)
    given = jnp.concatenate([given, jnp.broadcast_to(rest[None], (owners // 2,) + rest.shape)], axis=2)
    both = kept + lax.ppermute(given, "core", [(0, 1), (1, 0)])
    arrived = lax.all_to_all(both, "y", split_axis=0, concat_axis=0, tiled=True)

    near = sent - me * blk
    pick = jnp.max(jnp.where((near >= 0) & (near < blk), near, 0), axis=1)
    squares = jnp.sum(jnp.square(fine_cents.astype(jnp.float32)), axis=2, keepdims=True)
    least = nearest(after(pick, both), fine_cents, squares, rows)[:, 0]

    both_sum = jnp.sum(after(arrived, least), axis=0)
    fine_sum = both_sum[:, :full].reshape(blk, share, width)
    rest = both_sum[:, full:]
    mine = jnp.concatenate([rest[:chunk, :half], rest[chunk:, :half], rest[:chunk, half:]], axis=1)
    totals = lax.all_to_all(
        jnp.broadcast_to(mine[None], (planes,) + mine.shape), DP, split_axis=0, concat_axis=0, tiled=True
    ).reshape(COARSE, width + per)
    back = lax.all_gather(after(least, mine), CENT, axis=0, tiled=False)
    back = lax.dynamic_index_in_dim(back, me, 1, keepdims=False)
    totals = after(totals, back)
    counts = totals[:, width:]
    new_coarse = (anchor_coarse * coarse_cents + totals[:, :width]) / (
        anchor_coarse + jnp.sum(counts, axis=1, keepdims=True)
    )
    first = lax.axis_index(DP) * share
    former = lax.dynamic_slice_in_dim(fine_cents, first, share, 1).astype(jnp.float32)
    fine_num = lax.dynamic_slice(counts, (me * blk, first), (blk, share))
    new_fine = (anchor_fine * former + fine_sum) / (anchor_fine + fine_num[:, :, None])

    row_sq = jnp.sum(jnp.square(embeds.astype(jnp.float32)), axis=1)
    at = (coarse_ids // blk)[None, :] == jnp.arange(owners, dtype=jnp.int32)[:, None]
    gaps = (row_sq + jnp.sum(jnp.where(at, back, 0.0), axis=0)) / width
    return (new_fine, new_coarse, gaps)


def solution(mesh):
    fine_mesh = Mesh(mesh.devices.reshape(8, 4, 8, 2), DP + CENT)
    placed = (P(DP + CENT, None), P(DP + CENT), P(DP + CENT), P(), P(CENT, None, None))
    return jax.shard_map(
        body,
        mesh=fine_mesh,
        in_specs=placed,
        out_specs=(P(CENT, DP, None), P(), P(DP + CENT)),
        check_vma=False,
    )
```

```python
import functools

import jax
import jax.numpy as jnp
from jax import lax
from jax.experimental import pallas as pl
from jax.experimental.pallas import tpu as pltpu
from jax.sharding import Mesh, PartitionSpec as P

COARSE = 128
DP = ("z", "x")
CENT = ("y", "core")
STEPS = 13
VMEM = 56 * 2**20


def message_kernel(share, owned, coarse_ref, fine_ref, rows_ref, out_ref):
    count, width = rows_ref.shape
    per = 128
    lines = out_ref.shape[0]
    slots = 8
    coarse = coarse_ref[...]
    local = fine_ref[...] - coarse * per
    owner = coarse // owned

    owners = lax.broadcasted_iota(jnp.int32, (16, count), 0)
    present = jnp.max((owners == owner).astype(jnp.int32), axis=1, keepdims=True)
    slot_row = jnp.sum(jnp.where(owners < owner, present, 0), axis=0, keepdims=True)
    slot_ids = lax.broadcasted_iota(jnp.int32, (slots, count), 0)
    cluster = jnp.max(jnp.where(slot_ids == slot_row, coarse, 0), axis=1, keepdims=True)

    largest = jnp.max(jnp.abs(rows_ref[...]).astype(jnp.float32))
    scale, step = 1.0, 0.0
    for k in range(1, STEPS):
        fits = largest * 256.0**k <= 60000.0 / count
        scale = jnp.where(fits, 256.0**k, scale)
        step = jnp.where(fits, float(k), step)

    line = lax.broadcasted_iota(jnp.int32, (lines, 1), 0)
    key = slot_row * per + local
    target = (line % slots) * per + (line // slots) * share
    lane = lax.broadcasted_iota(jnp.int32, (lines, per), 1) % (per // 2)
    ones = jnp.ones((count, per), jnp.bfloat16)
    notes = jnp.broadcast_to(step, (lines, per))
    for j in range(share):
        hot = (target + j == key).astype(jnp.bfloat16)
        part = jnp.dot(hot, rows_ref[...], preferred_element_type=jnp.float32)
        out_ref[:, j * width : (j + 1) * width] = part * scale
        notes = jnp.where(lane == j, jnp.dot(hot, ones, preferred_element_type=jnp.float32), notes)
    hot = (slot_ids == slot_row).astype(jnp.bfloat16)
    part = jnp.dot(hot, rows_ref[...], preferred_element_type=jnp.float32) * scale
    number = jnp.dot(hot, ones, preferred_element_type=jnp.float32)
    cluster = jnp.broadcast_to(cluster.astype(jnp.float32), (slots, per))

    def spread(piece):
        whole = jnp.broadcast_to(piece[None], (lines // slots,) + piece.shape)
        return whole.reshape(lines, piece.shape[1])

    notes = jnp.where(lane == share, spread(number), jnp.where(lane == share + 1, spread(cluster), notes))
    out_ref[:, share * width : (share + 1) * width] = spread(part)
    out_ref[:, (share + 1) * width :] = notes


def message_of(coarse_ids, fine_ids, rows, planes, share, owned):
    width = rows.shape[1]
    shape = (planes * 8, (share + 1) * width + 128)
    return pl.pallas_call(
        functools.partial(message_kernel, share, owned),
        in_specs=[pl.BlockSpec(memory_space=pltpu.VMEM)] * 3,
        out_specs=pl.BlockSpec(memory_space=pltpu.VMEM),
        out_shape=jax.ShapeDtypeStruct(shape, jnp.float32),
        compiler_params=pltpu.CompilerParams(vmem_limit_bytes=VMEM),
        cost_estimate=pl.CostEstimate(
            flops=2 * shape[0] * shape[1] * rows.shape[0], bytes_accessed=16 * rows.size, transcendentals=0
        ),
    )(coarse_ids[None, :], fine_ids[None, :], rows)


def gaps_kernel(pick_ref, cents_ref, square_ref, rows_ref, out_ref, held, sems):
    sources = rows_ref.shape[0]

    def fetch(s):
        return pltpu.make_async_copy(rows_ref.at[s], held.at[s], sems.at[s])

    for s in range(sources):
        fetch(s).start()

    @pl.loop(0, sources, unroll=4)
    def _(s):
        c = pick_ref[s]
        fetch(s).wait()
        dots = lax.dot_general(
            cents_ref[c], held[s], (((1,), (1,)), ((), ())), preferred_element_type=jnp.float32
        )
        out_ref[s] = jnp.min(square_ref[c] - 2.0 * dots, axis=0, keepdims=True)


def nearest(pick, cents, squares, rows):
    sources, per_source, width = rows.shape
    return pl.pallas_call(
        gaps_kernel,
        in_specs=[
            pl.BlockSpec(memory_space=pltpu.SMEM),
            pl.BlockSpec(memory_space=pltpu.VMEM),
            pl.BlockSpec(memory_space=pltpu.VMEM),
            pl.BlockSpec(memory_space=pl.ANY),
        ],
        out_specs=pl.BlockSpec(memory_space=pltpu.VMEM),
        out_shape=jax.ShapeDtypeStruct((sources, 1, per_source), jnp.float32),
        scratch_shapes=[
            pltpu.VMEM(rows.shape, rows.dtype),
            pltpu.SemaphoreType.DMA((sources,)),
        ],
        compiler_params=pltpu.CompilerParams(vmem_limit_bytes=VMEM),
        cost_estimate=pl.CostEstimate(
            flops=2 * cents.shape[1] * rows.size, bytes_accessed=2 * rows.size, transcendentals=0
        ),
    )(pick, cents, squares, rows)


def settle_kernel(per, anchors, arrived_ref, fine_ref, coarse_ref, least_ref, new_fine_ref, news_ref):
    blocks, lines, columns = arrived_ref.shape
    wide = columns - per
    width = coarse_ref.shape[1]
    share = wide // width - 1
    factors = []
    notes = jnp.zeros((lines, per), jnp.float32)
    for y in range(blocks):
        step = arrived_ref[y, :1, wide:][:, per - 1 :]
        factor = jnp.full_like(step, 16.0)
        for k in range(1, STEPS):
            factor = jnp.where(step == k, 16.0 * 256.0**-k, factor)
        factors.append(factor)
        notes += arrived_ref[y, :, wide:]

    def total(j):
        at = pl.ds(j * width, width)
        found = arrived_ref[0, :, at] * factors[0]
        for y in range(1, blocks):
            found += arrived_ref[y, :, at] * factors[y]
        number = 64.0 * notes[:, j : j + 1] + notes[:, per // 2 + j : per // 2 + j + 1]
        return found, number

    found, number = total(share)
    ours = (anchors[0] * coarse_ref[...] + found) / (anchors[0] + number)
    sources, count = least_ref.shape
    half = lines // 2
    news_ref[:sources] = least_ref[...]
    news_ref[sources : sources + lines] = ours[:, :count]
    news_ref[sources + lines :] = jnp.concatenate([ours[:half, count:], ours[half:, count:]], axis=1)
    for j in range(share):
        found, number = total(j)
        new_fine_ref[:, j, :] = (anchors[1] * fine_ref[:, pl.ds(j * width, width)] + found) / (anchors[1] + number)


def settle(arrived, fine, coarse, least, per, anchors):
    lines, width = coarse.shape
    sources, count = least.shape
    return pl.pallas_call(
        functools.partial(settle_kernel, per, anchors),
        in_specs=[pl.BlockSpec(memory_space=pltpu.VMEM)] * 4,
        out_specs=[pl.BlockSpec(memory_space=pltpu.VMEM)] * 2,
        out_shape=[
            jax.ShapeDtypeStruct((lines, fine.shape[1] // width, width), jnp.float32),
            jax.ShapeDtypeStruct((sources + lines + lines // 2, count), jnp.float32),
        ],
        compiler_params=pltpu.CompilerParams(vmem_limit_bytes=VMEM),
    )(arrived, fine, coarse, least)


def after(value, earlier):
    return value + (earlier[(0,) * earlier.ndim].astype(jnp.float32) * 0.0).astype(value.dtype)


def power(step):
    up, down = jnp.ones_like(step), jnp.ones_like(step)
    for k in range(1, STEPS):
        up = jnp.where(step == k, 256.0**k, up)
        down = jnp.where(step == k, 256.0**-k, down)
    return up, down


def join_kernel(per, kept_ref, got_ref, out_ref):
    blocks, lines, columns = kept_ref.shape
    wide = columns - per
    lane = lax.broadcasted_iota(jnp.int32, (lines, per), 1)
    step = jnp.minimum(kept_ref[0, :1, wide:], got_ref[0, :1, wide:])[:, per - 1 :]
    scale = power(step)[0] * 0.0625
    for y in range(blocks):
        out_ref[y, :, :wide] = (kept_ref[y, :, :wide] + got_ref[y, :, :wide]) * scale
        notes = kept_ref[y, :, wide:] + got_ref[y, :, wide:]
        high = jnp.floor(notes * (1.0 / 64.0))
        notes = jnp.where(lane < per // 2, high, notes - 64.0 * high)
        out_ref[y, :, wide:] = jnp.where(lane == per - 1, jnp.broadcast_to(step, notes.shape), notes)


def join(kept, got, per):
    return pl.pallas_call(
        functools.partial(join_kernel, per),
        in_specs=[pl.BlockSpec(memory_space=pltpu.VMEM)] * 2,
        out_specs=pl.BlockSpec(memory_space=pltpu.VMEM),
        out_shape=jax.ShapeDtypeStruct(kept.shape, jnp.float32),
        compiler_params=pltpu.CompilerParams(vmem_limit_bytes=VMEM),
    )(kept, got)


def body(embeds, coarse_ids, fine_ids, coarse_cents, fine_cents):
    blk, per, width = fine_cents.shape
    count = embeds.shape[0]
    planes = lax.axis_size(DP)
    owners = lax.axis_size(CENT)
    share = per // planes
    slots = 8
    me = lax.axis_index(CENT)
    core = lax.axis_index("core")
    anchor_coarse = count * planes * owners // COARSE
    anchor_fine = max(1, anchor_coarse // per)

    rows = lax.all_gather(embeds, CENT, axis=0, tiled=False)

    message = message_of(coarse_ids, fine_ids, embeds, planes, share, blk)
    heard = message.astype(jnp.float16).reshape(planes, slots, -1)
    heard = lax.all_to_all(heard, DP, split_axis=0, concat_axis=0, tiled=True)
    sent = lax.all_gather(after(coarse_ids, message), CENT, axis=0, tiled=False)

    near = sent - me * blk
    pick = jnp.max(jnp.where((near >= 0) & (near < blk), near, 0), axis=1)
    squares = jnp.sum(jnp.square(fine_cents.astype(jnp.float32)), axis=2, keepdims=True)
    first = lax.axis_index(DP) * share
    fine = lax.dynamic_slice_in_dim(fine_cents, first, share, 1).astype(jnp.float32).reshape(blk, share * width)
    coarse = lax.dynamic_slice_in_dim(coarse_cents, me * blk, blk, 0)
    wide = (share + 1) * width
    notes = heard[:, :, wide:].astype(jnp.float32)
    for ready in (pick, squares, fine, coarse):
        notes = after(notes, ready)
    step = notes[:, 0, per - 1]
    found = jnp.arange(COARSE, dtype=jnp.float32)[:, None, None] == notes[None, :, :, share + 1]
    weights = jnp.where(found, jnp.exp2(-8.0 * step)[None, :, None], 0.0)
    weights = weights.reshape(COARSE, planes * slots).astype(jnp.bfloat16)
    values = heard[:, :, :wide].reshape(planes * slots, wide).astype(jnp.float32)
    high = lax.reduce_precision(values, 8, 7)
    low = (values - high).astype(jnp.bfloat16)
    table = jnp.dot(weights, high.astype(jnp.bfloat16), preferred_element_type=jnp.float32)
    table = table + jnp.dot(weights, low, preferred_element_type=jnp.float32)
    plain = found.reshape(COARSE, planes * slots).astype(jnp.bfloat16)
    notes = notes.reshape(planes * slots, per).astype(jnp.bfloat16)
    notes = jnp.dot(plain, notes, preferred_element_type=jnp.float32)
    notes = jnp.where(jnp.arange(per, dtype=jnp.int32)[None, :] == per - 1, jnp.min(step), notes)

    table = jnp.concatenate([table, notes], axis=1).reshape(owners // 2, 2, blk, wide + per)
    kept = lax.dynamic_index_in_dim(table, core, 1, keepdims=False)
    given = lax.dynamic_index_in_dim(table, 1 - core, 1, keepdims=False)
    got = lax.ppermute(given, "core", [(0, 1), (1, 0)])
    both = join(kept, got, per).astype(jnp.float16)
    arrived = lax.all_to_all(both, "y", split_axis=0, concat_axis=0, tiled=True)
    least = nearest(after(pick, both), fine_cents, squares, rows)[:, 0]
    arrived = after(arrived.astype(jnp.float32), least)
    anchors = (float(anchor_coarse), float(anchor_fine))
    new_fine, news = settle(arrived, fine, coarse, least, per, anchors)

    news = lax.all_gather(news, CENT, axis=0, tiled=False)
    tails = news[:, owners + blk :]
    tails = jnp.concatenate([tails[:, :, : width - count], tails[:, :, width - count :]], axis=1)
    new_coarse = jnp.concatenate([news[:, owners : owners + blk], tails], axis=2).reshape(COARSE, width)
    back = lax.dynamic_index_in_dim(news, me, 1, keepdims=False)
    row_sq = jnp.sum(jnp.square(embeds.astype(jnp.float32)), axis=1)
    at = (coarse_ids // blk)[None, :] == jnp.arange(owners, dtype=jnp.int32)[:, None]
    gaps = (row_sq + jnp.sum(jnp.where(at, back, 0.0), axis=0)) / width
    return (new_fine, new_coarse, gaps)


def solution(mesh):
    fine_mesh = Mesh(mesh.devices.reshape(8, 4, 8, 2), DP + CENT)
    placed = (P(DP + CENT, None), P(DP + CENT), P(DP + CENT), P(), P(CENT, None, None))
    return jax.shard_map(
        body,
        mesh=fine_mesh,
        in_specs=placed,
        out_specs=(P(CENT, DP, None), P(), P(DP + CENT)),
        check_vma=False,
    )
```

```python
import functools

import jax
import jax.numpy as jnp
from jax import lax
from jax.experimental import pallas as pl
from jax.experimental.pallas import tpu as pltpu
from jax.sharding import Mesh, PartitionSpec as P

COARSE = 128
DP = ("z", "x")
CENT = ("y", "core")
STEPS = 13
SMALL = 16 * 2**20
LARGE = 56 * 2**20


def message_kernel(share, owned, coarse_ref, fine_ref, rows_ref, out_ref):
    count, width = rows_ref.shape
    per = 128
    lines = out_ref.shape[0]
    slots = 8
    coarse = coarse_ref[...]
    local = fine_ref[...] - coarse * per
    owner = coarse // owned

    owners = lax.broadcasted_iota(jnp.int32, (16, count), 0)
    present = jnp.max((owners == owner).astype(jnp.int32), axis=1, keepdims=True)
    slot_row = jnp.sum(jnp.where(owners < owner, present, 0), axis=0, keepdims=True)
    slot_ids = lax.broadcasted_iota(jnp.int32, (slots, count), 0)
    cluster = jnp.max(jnp.where(slot_ids == slot_row, coarse, 0), axis=1, keepdims=True)

    largest = jnp.max(jnp.abs(rows_ref[...]).astype(jnp.float32))
    scale, step = 1.0, 0.0
    for k in range(1, STEPS):
        fits = largest * 256.0**k <= 60000.0 / count
        scale = jnp.where(fits, 256.0**k, scale)
        step = jnp.where(fits, float(k), step)

    line = lax.broadcasted_iota(jnp.int32, (lines, 1), 0)
    key = slot_row * per + local
    target = (line % slots) * per + (line // slots) * share
    lane = lax.broadcasted_iota(jnp.int32, (lines, per), 1) % (per // 2)
    ones = jnp.ones((count, per), jnp.bfloat16)
    notes = jnp.broadcast_to(step, (lines, per))
    for j in range(share):
        hot = (target + j == key).astype(jnp.bfloat16)
        part = jnp.dot(hot, rows_ref[...], preferred_element_type=jnp.float32)
        out_ref[:, j * width : (j + 1) * width] = part * scale
        notes = jnp.where(lane == j, jnp.dot(hot, ones, preferred_element_type=jnp.float32), notes)
    hot = (slot_ids == slot_row).astype(jnp.bfloat16)
    part = jnp.dot(hot, rows_ref[...], preferred_element_type=jnp.float32) * scale
    number = jnp.dot(hot, ones, preferred_element_type=jnp.float32)
    cluster = jnp.broadcast_to(cluster.astype(jnp.float32), (slots, per))

    def spread(piece):
        whole = jnp.broadcast_to(piece[None], (lines // slots,) + piece.shape)
        return whole.reshape(lines, piece.shape[1])

    notes = jnp.where(lane == share, spread(number), jnp.where(lane == share + 1, spread(cluster), notes))
    out_ref[:, share * width : (share + 1) * width] = spread(part)
    out_ref[:, (share + 1) * width :] = notes


def message_of(coarse_ids, fine_ids, rows, planes, share, owned):
    width = rows.shape[1]
    shape = (planes * 8, (share + 1) * width + 128)
    return pl.pallas_call(
        functools.partial(message_kernel, share, owned),
        in_specs=[pl.BlockSpec(memory_space=pltpu.VMEM)] * 3,
        out_specs=pl.BlockSpec(memory_space=pltpu.VMEM),
        out_shape=jax.ShapeDtypeStruct(shape, jnp.float32),
        compiler_params=pltpu.CompilerParams(vmem_limit_bytes=SMALL),
        cost_estimate=pl.CostEstimate(
            flops=2 * shape[0] * shape[1] * rows.shape[0], bytes_accessed=16 * rows.size, transcendentals=0
        ),
    )(coarse_ids[None, :], fine_ids[None, :], rows)


def gaps_kernel(pick_ref, cents_ref, square_ref, rows_ref, out_ref, held, sems):
    sources = rows_ref.shape[0]

    def fetch(s):
        return pltpu.make_async_copy(rows_ref.at[s], held.at[s], sems.at[s])

    for s in range(sources):
        fetch(s).start()

    @pl.loop(0, sources, unroll=4)
    def _(s):
        c = pick_ref[s]
        fetch(s).wait()
        dots = lax.dot_general(
            cents_ref[c], held[s], (((1,), (1,)), ((), ())), preferred_element_type=jnp.float32
        )
        out_ref[s] = jnp.min(square_ref[c] - 2.0 * dots, axis=0, keepdims=True)


def nearest(pick, cents, squares, rows):
    sources, per_source, width = rows.shape
    return pl.pallas_call(
        gaps_kernel,
        in_specs=[
            pl.BlockSpec(memory_space=pltpu.SMEM),
            pl.BlockSpec(memory_space=pltpu.VMEM),
            pl.BlockSpec(memory_space=pltpu.VMEM),
            pl.BlockSpec(memory_space=pl.ANY),
        ],
        out_specs=pl.BlockSpec(memory_space=pltpu.VMEM),
        out_shape=jax.ShapeDtypeStruct((sources, 1, per_source), jnp.float32),
        scratch_shapes=[
            pltpu.VMEM(rows.shape, rows.dtype),
            pltpu.SemaphoreType.DMA((sources,)),
        ],
        compiler_params=pltpu.CompilerParams(vmem_limit_bytes=LARGE),
        cost_estimate=pl.CostEstimate(
            flops=2 * cents.shape[1] * rows.size, bytes_accessed=2 * rows.size, transcendentals=0
        ),
    )(pick, cents, squares, rows)


def settle_kernel(per, anchors, arrived_ref, fine_ref, coarse_ref, least_ref, new_fine_ref, news_ref):
    blocks, lines, columns = arrived_ref.shape
    wide = columns - per
    width = coarse_ref.shape[1]
    share = wide // width - 1
    factors = []
    notes = jnp.zeros((lines, per), jnp.float32)
    for y in range(blocks):
        step = arrived_ref[y, :1, wide:][:, per - 1 :]
        factor = jnp.full_like(step, 16.0)
        for k in range(1, STEPS):
            factor = jnp.where(step == k, 16.0 * 256.0**-k, factor)
        factors.append(factor)
        notes += arrived_ref[y, :, wide:]

    def total(j):
        at = pl.ds(j * width, width)
        found = arrived_ref[0, :, at] * factors[0]
        for y in range(1, blocks):
            found += arrived_ref[y, :, at] * factors[y]
        number = 64.0 * notes[:, j : j + 1] + notes[:, per // 2 + j : per // 2 + j + 1]
        return found, number

    found, number = total(share)
    ours = (anchors[0] * coarse_ref[...] + found) / (anchors[0] + number)
    sources, count = least_ref.shape
    half = lines // 2
    news_ref[:sources] = least_ref[...]
    news_ref[sources : sources + lines] = ours[:, :count]
    news_ref[sources + lines :] = jnp.concatenate([ours[:half, count:], ours[half:, count:]], axis=1)
    for j in range(share):
        found, number = total(j)
        new_fine_ref[:, j, :] = (anchors[1] * fine_ref[:, pl.ds(j * width, width)] + found) / (anchors[1] + number)


def settle(arrived, fine, coarse, least, per, anchors):
    lines, width = coarse.shape
    sources, count = least.shape
    return pl.pallas_call(
        functools.partial(settle_kernel, per, anchors),
        in_specs=[pl.BlockSpec(memory_space=pltpu.VMEM)] * 4,
        out_specs=[pl.BlockSpec(memory_space=pltpu.VMEM)] * 2,
        out_shape=[
            jax.ShapeDtypeStruct((lines, fine.shape[1] // width, width), jnp.float32),
            jax.ShapeDtypeStruct((sources + lines + lines // 2, count), jnp.float32),
        ],
        compiler_params=pltpu.CompilerParams(vmem_limit_bytes=SMALL),
    )(arrived, fine, coarse, least)


def after(value, earlier):
    return value + (earlier[(0,) * earlier.ndim].astype(jnp.float32) * 0.0).astype(value.dtype)


def power(step):
    up, down = jnp.ones_like(step), jnp.ones_like(step)
    for k in range(1, STEPS):
        up = jnp.where(step == k, 256.0**k, up)
        down = jnp.where(step == k, 256.0**-k, down)
    return up, down


def join_kernel(per, kept_ref, got_ref, out_ref):
    blocks, lines, columns = kept_ref.shape
    wide = columns - per
    lane = lax.broadcasted_iota(jnp.int32, (lines, per), 1)
    step = jnp.minimum(kept_ref[0, :1, wide:], got_ref[0, :1, wide:])[:, per - 1 :]
    scale = power(step)[0] * 0.0625
    for y in range(blocks):
        out_ref[y, :, :wide] = (kept_ref[y, :, :wide] + got_ref[y, :, :wide]) * scale
        notes = kept_ref[y, :, wide:] + got_ref[y, :, wide:]
        high = jnp.floor(notes * (1.0 / 64.0))
        notes = jnp.where(lane < per // 2, high, notes - 64.0 * high)
        out_ref[y, :, wide:] = jnp.where(lane == per - 1, jnp.broadcast_to(step, notes.shape), notes)


def join(kept, got, per):
    return pl.pallas_call(
        functools.partial(join_kernel, per),
        in_specs=[pl.BlockSpec(memory_space=pltpu.VMEM)] * 2,
        out_specs=pl.BlockSpec(memory_space=pltpu.VMEM),
        out_shape=jax.ShapeDtypeStruct(kept.shape, jnp.float32),
        compiler_params=pltpu.CompilerParams(vmem_limit_bytes=SMALL),
    )(kept, got)


def body(embeds, coarse_ids, fine_ids, coarse_cents, fine_cents):
    blk, per, width = fine_cents.shape
    count = embeds.shape[0]
    planes = lax.axis_size(DP)
    owners = lax.axis_size(CENT)
    share = per // planes
    slots = 8
    me = lax.axis_index(CENT)
    core = lax.axis_index("core")
    anchor_coarse = count * planes * owners // COARSE
    anchor_fine = max(1, anchor_coarse // per)

    rows = lax.all_gather(embeds, CENT, axis=0, tiled=False)

    message = message_of(coarse_ids, fine_ids, embeds, planes, share, blk)
    heard = message.astype(jnp.float16).reshape(planes, slots, -1)
    heard = lax.all_to_all(heard, DP, split_axis=0, concat_axis=0, tiled=True)
    sent = lax.all_gather(after(coarse_ids, message), CENT, axis=0, tiled=False)

    near = sent - me * blk
    pick = jnp.max(jnp.where((near >= 0) & (near < blk), near, 0), axis=1)
    squares = jnp.sum(jnp.square(fine_cents.astype(jnp.float32)), axis=2, keepdims=True)
    first = lax.axis_index(DP) * share
    fine = lax.dynamic_slice_in_dim(fine_cents, first, share, 1).astype(jnp.float32).reshape(blk, share * width)
    coarse = lax.dynamic_slice_in_dim(coarse_cents, me * blk, blk, 0)
    wide = (share + 1) * width
    notes = heard[:, :, wide:].astype(jnp.float32)
    for ready in (pick, squares, fine, coarse):
        notes = after(notes, ready)
    step = notes[:, 0, per - 1]
    found = jnp.arange(COARSE, dtype=jnp.float32)[:, None, None] == notes[None, :, :, share + 1]
    weights = jnp.where(found, jnp.exp2(-8.0 * step)[None, :, None], 0.0)
    weights = weights.reshape(COARSE, planes * slots).astype(jnp.bfloat16)
    values = heard[:, :, :wide].reshape(planes * slots, wide).astype(jnp.float32)
    high = lax.reduce_precision(values, 8, 7)
    low = (values - high).astype(jnp.bfloat16)
    table = jnp.dot(weights, high.astype(jnp.bfloat16), preferred_element_type=jnp.float32)
    table = table + jnp.dot(weights, low, preferred_element_type=jnp.float32)
    plain = found.reshape(COARSE, planes * slots).astype(jnp.bfloat16)
    notes = notes.reshape(planes * slots, per).astype(jnp.bfloat16)
    notes = jnp.dot(plain, notes, preferred_element_type=jnp.float32)
    notes = jnp.where(jnp.arange(per, dtype=jnp.int32)[None, :] == per - 1, jnp.min(step), notes)

    table = jnp.concatenate([table, notes], axis=1).reshape(owners // 2, 2, blk, wide + per)
    kept = lax.dynamic_index_in_dim(table, core, 1, keepdims=False)
    given = lax.dynamic_index_in_dim(table, 1 - core, 1, keepdims=False)
    got = lax.ppermute(given, "core", [(0, 1), (1, 0)])
    both = join(kept, got, per).astype(jnp.float16)
    arrived = lax.all_to_all(both, "y", split_axis=0, concat_axis=0, tiled=True)
    least = nearest(after(pick, both), fine_cents, squares, rows)[:, 0]
    arrived = after(arrived.astype(jnp.float32), least)
    anchors = (float(anchor_coarse), float(anchor_fine))
    new_fine, news = settle(arrived, fine, coarse, least, per, anchors)

    news = lax.all_gather(news, CENT, axis=0, tiled=False)
    tails = news[:, owners + blk :]
    tails = jnp.concatenate([tails[:, :, : width - count], tails[:, :, width - count :]], axis=1)
    new_coarse = jnp.concatenate([news[:, owners : owners + blk], tails], axis=2).reshape(COARSE, width)
    back = lax.dynamic_index_in_dim(news, me, 1, keepdims=False)
    row_sq = jnp.sum(jnp.square(embeds.astype(jnp.float32)), axis=1)
    at = (coarse_ids // blk)[None, :] == jnp.arange(owners, dtype=jnp.int32)[:, None]
    gaps = (row_sq + jnp.sum(jnp.where(at, back, 0.0), axis=0)) / width
    return (new_fine, new_coarse, gaps)


def solution(mesh):
    fine_mesh = Mesh(mesh.devices.reshape(8, 4, 8, 2), DP + CENT)
    placed = (P(DP + CENT, None), P(DP + CENT), P(DP + CENT), P(), P(CENT, None, None))
    return jax.shard_map(
        body,
        mesh=fine_mesh,
        in_specs=placed,
        out_specs=(P(CENT, DP, None), P(), P(DP + CENT)),
        check_vma=False,
    )
```

```python
import functools

import jax
import jax.numpy as jnp
from jax import lax
from jax.experimental import pallas as pl
from jax.experimental.pallas import tpu as pltpu
from jax.sharding import Mesh, PartitionSpec as P

COARSE = 128
DP = ("z", "x")
CENT = ("y", "core")
STEPS = 13
SMALL = 16 * 2**20
LARGE = 56 * 2**20


def message_kernel(share, owned, fine_ref, rows_ref, out_ref):
    count, width = rows_ref.shape
    per = 128
    lines = out_ref.shape[0]
    slots = 8
    coarse = fine_ref[...] // per
    local = fine_ref[...] % per
    owner = coarse // owned

    owners = lax.broadcasted_iota(jnp.int32, (16, count), 0)
    present = jnp.max((owners == owner).astype(jnp.int32), axis=1, keepdims=True)
    slot_row = jnp.sum(jnp.where(owners < owner, present, 0), axis=0, keepdims=True)
    slot_ids = lax.broadcasted_iota(jnp.int32, (slots, count), 0)
    cluster = jnp.max(jnp.where(slot_ids == slot_row, coarse, 0), axis=1, keepdims=True)

    largest = jnp.max(jnp.abs(rows_ref[...]).astype(jnp.float32))
    scale, step = 1.0, 0.0
    for k in range(1, STEPS):
        fits = largest * 256.0**k <= 60000.0 / count
        scale = jnp.where(fits, 256.0**k, scale)
        step = jnp.where(fits, float(k), step)

    line = lax.broadcasted_iota(jnp.int32, (lines, 1), 0)
    key = slot_row * per + local
    target = (line % slots) * per + (line // slots) * share
    lane = lax.broadcasted_iota(jnp.int32, (lines, per), 1) % (per // 2)
    ones = jnp.ones((count, per), jnp.bfloat16)
    notes = jnp.broadcast_to(step, (lines, per))
    for j in range(share):
        hot = (target + j == key).astype(jnp.bfloat16)
        part = jnp.dot(hot, rows_ref[...], preferred_element_type=jnp.float32)
        out_ref[:, j * width : (j + 1) * width] = part * scale
        notes = jnp.where(lane == j, jnp.dot(hot, ones, preferred_element_type=jnp.float32), notes)
    hot = (slot_ids == slot_row).astype(jnp.bfloat16)
    part = jnp.dot(hot, rows_ref[...], preferred_element_type=jnp.float32) * scale
    number = jnp.dot(hot, ones, preferred_element_type=jnp.float32)
    cluster = jnp.broadcast_to(cluster.astype(jnp.float32), (slots, per))

    def spread(piece):
        whole = jnp.broadcast_to(piece[None], (lines // slots,) + piece.shape)
        return whole.reshape(lines, piece.shape[1])

    notes = jnp.where(lane == share, spread(number), jnp.where(lane == share + 1, spread(cluster), notes))
    out_ref[:, share * width : (share + 1) * width] = spread(part)
    out_ref[:, (share + 1) * width :] = notes


def message_of(fine_ids, rows, planes, share, owned):
    width = rows.shape[1]
    shape = (planes * 8, (share + 1) * width + 128)
    return pl.pallas_call(
        functools.partial(message_kernel, share, owned),
        in_specs=[pl.BlockSpec(memory_space=pltpu.VMEM)] * 2,
        out_specs=pl.BlockSpec(memory_space=pltpu.VMEM),
        out_shape=jax.ShapeDtypeStruct(shape, jnp.float32),
        compiler_params=pltpu.CompilerParams(vmem_limit_bytes=SMALL),
        cost_estimate=pl.CostEstimate(
            flops=2 * shape[0] * shape[1] * rows.shape[0], bytes_accessed=16 * rows.size, transcendentals=0
        ),
    )(fine_ids[None, :], rows)


def gaps_kernel(pick_ref, cents_ref, square_ref, rows_ref, out_ref, held, sems):
    sources = rows_ref.shape[0]

    def fetch(s):
        return pltpu.make_async_copy(rows_ref.at[s], held.at[s], sems.at[s])

    for s in range(sources):
        fetch(s).start()

    @pl.loop(0, sources, unroll=4)
    def _(s):
        c = pick_ref[s]
        fetch(s).wait()
        dots = lax.dot_general(
            cents_ref[c], held[s], (((1,), (1,)), ((), ())), preferred_element_type=jnp.float32
        )
        out_ref[s] = jnp.min(square_ref[c] - 2.0 * dots, axis=0, keepdims=True)


def nearest(pick, cents, squares, rows):
    sources, per_source, width = rows.shape
    return pl.pallas_call(
        gaps_kernel,
        in_specs=[
            pl.BlockSpec(memory_space=pltpu.SMEM),
            pl.BlockSpec(memory_space=pltpu.VMEM),
            pl.BlockSpec(memory_space=pltpu.VMEM),
            pl.BlockSpec(memory_space=pl.ANY),
        ],
        out_specs=pl.BlockSpec(memory_space=pltpu.VMEM),
        out_shape=jax.ShapeDtypeStruct((sources, 1, per_source), jnp.float32),
        scratch_shapes=[
            pltpu.VMEM(rows.shape, rows.dtype),
            pltpu.SemaphoreType.DMA((sources,)),
        ],
        compiler_params=pltpu.CompilerParams(vmem_limit_bytes=LARGE),
        cost_estimate=pl.CostEstimate(
            flops=2 * cents.shape[1] * rows.size, bytes_accessed=2 * rows.size, transcendentals=0
        ),
    )(pick, cents, squares, rows)


def settle_kernel(per, anchors, arrived_ref, fine_ref, coarse_ref, least_ref, new_fine_ref, news_ref):
    blocks, lines, columns = arrived_ref.shape
    wide = columns - per
    width = coarse_ref.shape[1]
    share = wide // width - 1
    factors = []
    notes = jnp.zeros((lines, per), jnp.float32)
    for y in range(blocks):
        step = arrived_ref[y, :1, wide:][:, per - 1 :]
        factor = jnp.full_like(step, 16.0)
        for k in range(1, STEPS):
            factor = jnp.where(step == k, 16.0 * 256.0**-k, factor)
        factors.append(factor)
        notes += arrived_ref[y, :, wide:]

    def total(j):
        at = pl.ds(j * width, width)
        found = arrived_ref[0, :, at] * factors[0]
        for y in range(1, blocks):
            found += arrived_ref[y, :, at] * factors[y]
        number = 64.0 * notes[:, j : j + 1] + notes[:, per // 2 + j : per // 2 + j + 1]
        return found, number

    found, number = total(share)
    ours = (anchors[0] * coarse_ref[...] + found) / (anchors[0] + number)
    sources, count = least_ref.shape
    half = lines // 2
    news_ref[:sources] = least_ref[...]
    news_ref[sources : sources + lines] = ours[:, :count]
    news_ref[sources + lines :] = jnp.concatenate([ours[:half, count:], ours[half:, count:]], axis=1)
    for j in range(share):
        found, number = total(j)
        new_fine_ref[:, j, :] = (anchors[1] * fine_ref[:, pl.ds(j * width, width)] + found) / (anchors[1] + number)


def settle(arrived, fine, coarse, least, per, anchors):
    lines, width = coarse.shape
    sources, count = least.shape
    return pl.pallas_call(
        functools.partial(settle_kernel, per, anchors),
        in_specs=[pl.BlockSpec(memory_space=pltpu.VMEM)] * 4,
        out_specs=[pl.BlockSpec(memory_space=pltpu.VMEM)] * 2,
        out_shape=[
            jax.ShapeDtypeStruct((lines, fine.shape[1] // width, width), jnp.float32),
            jax.ShapeDtypeStruct((sources + lines + lines // 2, count), jnp.float32),
        ],
        compiler_params=pltpu.CompilerParams(vmem_limit_bytes=SMALL),
    )(arrived, fine, coarse, least)


def after(value, earlier):
    return value + (earlier[(0,) * earlier.ndim].astype(jnp.float32) * 0.0).astype(value.dtype)


def power(step):
    up, down = jnp.ones_like(step), jnp.ones_like(step)
    for k in range(1, STEPS):
        up = jnp.where(step == k, 256.0**k, up)
        down = jnp.where(step == k, 256.0**-k, down)
    return up, down


def join_kernel(per, kept_ref, got_ref, out_ref):
    blocks, lines, columns = kept_ref.shape
    wide = columns - per
    lane = lax.broadcasted_iota(jnp.int32, (lines, per), 1)
    step = jnp.minimum(kept_ref[0, :1, wide:], got_ref[0, :1, wide:])[:, per - 1 :]
    scale = power(step)[0] * 0.0625
    for y in range(blocks):
        out_ref[y, :, :wide] = (kept_ref[y, :, :wide] + got_ref[y, :, :wide]) * scale
        notes = kept_ref[y, :, wide:] + got_ref[y, :, wide:]
        high = jnp.floor(notes * (1.0 / 64.0))
        notes = jnp.where(lane < per // 2, high, notes - 64.0 * high)
        out_ref[y, :, wide:] = jnp.where(lane == per - 1, jnp.broadcast_to(step, notes.shape), notes)


def join(kept, got, per):
    return pl.pallas_call(
        functools.partial(join_kernel, per),
        in_specs=[pl.BlockSpec(memory_space=pltpu.VMEM)] * 2,
        out_specs=pl.BlockSpec(memory_space=pltpu.VMEM),
        out_shape=jax.ShapeDtypeStruct(kept.shape, jnp.float32),
        compiler_params=pltpu.CompilerParams(vmem_limit_bytes=SMALL),
    )(kept, got)


def body(embeds, coarse_ids, fine_ids, coarse_cents, fine_cents):
    blk, per, width = fine_cents.shape
    count = embeds.shape[0]
    planes = lax.axis_size(DP)
    owners = lax.axis_size(CENT)
    share = per // planes
    slots = 8
    me = lax.axis_index(CENT)
    core = lax.axis_index("core")
    anchor_coarse = count * planes * owners // COARSE
    anchor_fine = max(1, anchor_coarse // per)

    rows = lax.all_gather(embeds, CENT, axis=0, tiled=False)

    message = message_of(fine_ids, embeds, planes, share, blk)
    message = message.astype(jnp.float16).reshape(planes, slots, -1)
    heard = lax.all_to_all(message, DP, split_axis=0, concat_axis=0, tiled=True)
    sent = lax.all_gather(after(coarse_ids, message), CENT, axis=0, tiled=False)

    near = sent - me * blk
    pick = jnp.max(jnp.where((near >= 0) & (near < blk), near, 0), axis=1)
    squares = jnp.sum(jnp.square(fine_cents.astype(jnp.float32)), axis=2, keepdims=True)
    first = lax.axis_index(DP) * share
    fine = lax.dynamic_slice_in_dim(fine_cents, first, share, 1).astype(jnp.float32).reshape(blk, share * width)
    coarse = lax.dynamic_slice_in_dim(coarse_cents, me * blk, blk, 0)
    wide = (share + 1) * width
    notes = heard[:, :, wide:].astype(jnp.float32)
    for ready in (pick, squares, fine, coarse):
        notes = after(notes, ready)
    step = notes[:, 0, per - 1]
    found = jnp.arange(COARSE, dtype=jnp.float32)[:, None, None] == notes[None, :, :, share + 1]
    weights = jnp.where(found, jnp.exp2(-8.0 * step)[None, :, None], 0.0)
    weights = weights.reshape(COARSE, planes * slots).astype(jnp.bfloat16)
    values = heard[:, :, :wide].reshape(planes * slots, wide).astype(jnp.float32)
    high = lax.reduce_precision(values, 8, 7)
    low = (values - high).astype(jnp.bfloat16)
    table = jnp.dot(weights, high.astype(jnp.bfloat16), preferred_element_type=jnp.float32)
    table = table + jnp.dot(weights, low, preferred_element_type=jnp.float32)
    plain = found.reshape(COARSE, planes * slots).astype(jnp.bfloat16)
    notes = notes.reshape(planes * slots, per).astype(jnp.bfloat16)
    notes = jnp.dot(plain, notes, preferred_element_type=jnp.float32)
    notes = jnp.where(jnp.arange(per, dtype=jnp.int32)[None, :] == per - 1, jnp.min(step), notes)

    table = jnp.concatenate([table, notes], axis=1).reshape(owners // 2, 2, blk, wide + per)
    kept = lax.dynamic_index_in_dim(table, core, 1, keepdims=False)
    given = lax.dynamic_index_in_dim(table, 1 - core, 1, keepdims=False)
    got = lax.ppermute(given, "core", [(0, 1), (1, 0)])
    both = join(kept, got, per).astype(jnp.float16)
    arrived = lax.all_to_all(both, "y", split_axis=0, concat_axis=0, tiled=True)
    least = nearest(after(pick, both), fine_cents, squares, rows)[:, 0]
    arrived = after(arrived.astype(jnp.float32), least)
    anchors = (float(anchor_coarse), float(anchor_fine))
    new_fine, news = settle(arrived, fine, coarse, least, per, anchors)

    news = lax.all_gather(news, CENT, axis=0, tiled=False)
    tails = news[:, owners + blk :]
    tails = jnp.concatenate([tails[:, :, : width - count], tails[:, :, width - count :]], axis=1)
    new_coarse = jnp.concatenate([news[:, owners : owners + blk], tails], axis=2).reshape(COARSE, width)
    back = lax.dynamic_index_in_dim(news, me, 1, keepdims=False)
    row_sq = jnp.sum(jnp.square(embeds.astype(jnp.float32)), axis=1)
    at = (coarse_ids // blk)[None, :] == jnp.arange(owners, dtype=jnp.int32)[:, None]
    gaps = (row_sq + jnp.sum(jnp.where(at, back, 0.0), axis=0)) / width
    return (new_fine, new_coarse, gaps)


def solution(mesh):
    fine_mesh = Mesh(mesh.devices.reshape(8, 4, 8, 2), DP + CENT)
    placed = (P(DP + CENT, None), P(DP + CENT), P(DP + CENT), P(), P(CENT, None, None))
    return jax.shard_map(
        body,
        mesh=fine_mesh,
        in_specs=placed,
        out_specs=(P(CENT, DP, None), P(), P(DP + CENT)),
        check_vma=False,
    )
```
